768 devices in a mesh: dp: 24 (over z, x_lo), fsdp: 32 (over y, x_hi, core).
Axes of the slice: x: 4 (x_hi: 2, x_lo: 2; x = x_hi * 2 + x_lo), y: 8, z: 12, core: 2. Of those that a mesh axis runs over, the one named last changes fastest.
Arguments:
- tokens: bfloat16 [16384, 6144], P('fsdp'), may hold values from -6 to 6
- routes: int32 [16384, 2], P('fsdp'), may hold values from 0 to 7, as said below
- router_prob: float32 [16384, 2], P('fsdp'), may hold values from 0.1 to 1
- lengths: int32 [32, 8], P('fsdp'), may hold values from 1 to 96, 512 in all within a row
- pair_mask: int32 [32, 4], P('fsdp'), may hold values from 0 to 1, as said below
- margins: float32 [32, 4], P('fsdp'), may hold values from -8 to 8
- hidden_grad: bfloat16 [16384, 9216], P('fsdp', 'dp'), may hold values from -6 to 6
- gate_weight: bfloat16 [6144, 9216], P('fsdp', 'dp'), may hold values from -0.078125 to 0.078125
- up_weight: bfloat16 [6144, 9216], P('fsdp', 'dp'), may hold values from -0.078125 to 0.078125
Outputs:
- slot_grads: float32 [5120, 6144], P('fsdp', 'dp')
The draws below stay inside these ranges and needn't reach their ends.
Inputs may be any that keep to these rules, and one draw needn't show every extreme that they name: `routes`: no row names one expert twice. Among the 512 rows of one fsdp index, between 80 and 160 rows name expert 0, and on some index exactly 160. `pair_mask`: every fsdp index's row holds at least one 1.
All inputs are finite; a program needn't handle non-finite values.
Results may differ from the reference program's by a relative error of at most 0.0029.
Values may be sent and summed in bfloat16 or wider, within the bound.
No kernel may reach another device: no remote copies, remote signals or barrier semaphores. Data moves between devices by JAX's collectives and lax.ppermute only.
A program may use at most 64 MiB of HBM per device.

```python
import math
import jax
import jax.numpy as jnp
import numpy as np
from jax import lax

D = 6144
EXPERTS = 8
FF = 9216
TOK_DEV = 512
SEQ = 8
PAIRS = 4
CAP = 160
LEN_MOST = 96
TOKENS = 16384
N_FSDP = 32


def draw_routes(key, part):
    key = jax.random.fold_in(key, 11)
    blocks = TOKENS // TOK_DEV
    keys = jax.random.split(key, 6)
    counts = jax.random.randint(keys[0], (blocks,), CAP // 2, CAP + 1)
    full_block = jax.random.randint(keys[1], (), 0, blocks)
    counts = jnp.where(jnp.arange(blocks) == full_block, CAP, counts)
    scores = jax.random.randint(keys[2], (blocks, TOK_DEV), 0, 2 ** 20) * TOK_DEV + jnp.arange(TOK_DEV, dtype=jnp.int32)[None, :]
    ranks = jnp.argsort(jnp.argsort(scores, axis=1, stable=True), axis=1, stable=True)
    routed = (ranks < counts[:, None]).reshape(TOKENS)
    first = jax.random.randint(keys[3], (TOKENS,), 1, EXPERTS)
    offset = jax.random.randint(keys[4], (TOKENS,), 1, EXPERTS - 1)
    second = 1 + (first - 1 + offset) % (EXPERTS - 1)
    side = jax.random.randint(keys[5], (TOKENS,), 0, 2)
    column_one = jnp.where(routed, jnp.where(side == 0, 0, first), first)
    column_two = jnp.where(routed, jnp.where(side == 0, first, 0), second)
    return jnp.stack([column_one, column_two], axis=1).astype(jnp.int32)


def draw_pair_mask(key, part):
    key = jax.random.fold_in(key, 23)
    blocks = TOKENS // TOK_DEV
    keys = jax.random.split(key, 2)
    denom = 4 * max(blocks - 1, 1)
    levels = jax.random.randint(keys[0], (blocks, PAIRS), 0, denom)
    bounds = blocks - 1 + 2 * jnp.arange(blocks, dtype=jnp.int32)[:, None]
    forced = jax.random.randint(keys[1], (blocks, 1), 0, PAIRS)
    ones = (levels < bounds) | (jnp.arange(PAIRS, dtype=jnp.int32)[None, :] == forced)
    return ones.astype(jnp.int32)


def level_of(own_key, shape, shards, least, largest):
    factor_of, own = 1.0, jax.random.fold_in(own_key, 6)
    for position, blocks in shards:
        heights = jnp.exp(jax.random.uniform(jax.random.fold_in(own, position), (blocks,), jnp.float32, least / len(shards), largest / len(shards)))
        factor_of = factor_of * jnp.repeat(heights, shape[position] // blocks).reshape([-1 if axis == position else 1 for axis in range(len(shape))])
    return factor_of


def split_up(amount, total, most, lean):
    loads = [(1 << 20) // math.isqrt(standing ** lean) + 1 for standing in range(2, amount + 1)]
    surplus, given = total - most - (amount - 1), [1] * (amount - 1)
    while surplus > 0:
        free = [i for i in range(amount - 1) if given[i] < most]
        whole, left = sum([loads[i] for i in free]), surplus
        for i in free:
            addition = min(most - given[i], max(1, left * loads[i] // whole), surplus)
            given[i] = given[i] + addition
            surplus = surplus - addition
    return np.array([most] + given)


def uneven_parts(stream_key, number_of, total, reach, lean):
    if number_of == 2:
        one = jax.random.randint(stream_key, (), max(1, total - reach), min(reach, total - 1) + 1)
        return jnp.stack([one, total - one])
    sizes = jnp.asarray(split_up(number_of, total, reach, lean), jnp.int32)
    couples = (number_of - 1) // 2
    source_of, taker = sizes[1:1 + 2 * couples:2], sizes[2:2 + 2 * couples:2]
    room = jnp.minimum(source_of - 1, reach - taker)
    moved = jax.random.randint(jax.random.fold_in(stream_key, 1), (couples,), 0, 1 << 20) % (room + 1)
    sizes = sizes.at[1:1 + 2 * couples:2].set(source_of - moved).at[2:2 + 2 * couples:2].set(taker + moved)
    return sizes[jax.random.permutation(jax.random.fold_in(stream_key, 2), number_of)]


def scatter_about(stream_key, extent, deviation, reach, cuts=(), kind=jnp.bfloat16):
    result = jax.random.normal(stream_key, extent, jnp.float32) * deviation
    if len(cuts) > 0:
        result = level_of(stream_key, extent, cuts, -0.22, 0.18) * result
    return jnp.clip(result, min=-reach, max=reach).astype(kind)


def setup_inputs(seed: int = 0) -> dict:
    streams_of = jax.random.split(jax.random.key(seed), 10)
    tokens = scatter_about(streams_of[0], (TOKENS, D), 1.0, 6.0, ((0, 32),))
    routes = draw_routes(jax.random.fold_in(streams_of[9], 71), 0)
    router_prob = jnp.clip(jnp.exp(math.log(1.0) - 2.3025851 * jax.random.uniform(streams_of[2], (TOKENS, 2), jnp.float32) ** level_of(streams_of[2], (TOKENS, 2), ((0, 32),), -0.2, 0.2)), 0.1, 1.0)
    lengths = jax.vmap(lambda own: uneven_parts(own, SEQ, TOK_DEV, LEN_MOST, 1))(jax.random.split(streams_of[3], N_FSDP)).reshape((N_FSDP, SEQ)).astype(jnp.int32)
    pair_mask = draw_pair_mask(jax.random.fold_in(streams_of[9], 71), 0)
    margins = scatter_about(streams_of[5], (N_FSDP, PAIRS), 2.0, 8.0, ((0, 32),), jnp.float32)
    hidden_grad = scatter_about(streams_of[6], (TOKENS, FF), 1.0, 6.0, ((0, 32), (1, 24)))
    gate_weight = scatter_about(streams_of[7], (D, FF), D ** -0.5, 0.078125, ((0, 32), (1, 24)))
    up_weight = scatter_about(streams_of[8], (D, FF), D ** -0.5, 0.078125, ((0, 32), (1, 24)))
    return dict(tokens=tokens, routes=routes, router_prob=router_prob, lengths=lengths, pair_mask=pair_mask, margins=margins, hidden_grad=hidden_grad, gate_weight=gate_weight, up_weight=up_weight)


def slot_table(route_rows, capacity):
    count_rows = route_rows.shape[0]
    routed = jnp.any(route_rows == 0, axis=1)
    slot_of = jnp.cumsum(routed.astype(jnp.int32)) - 1
    slots = jnp.arange(capacity, dtype=jnp.int32)
    matches = (slot_of[None, :] == slots[:, None]) & routed[None, :]
    positions = jnp.arange(count_rows, dtype=jnp.int32)
    source_rows = jnp.sum(jnp.where(matches, positions[None, :], 0), axis=1).astype(jnp.int32)
    filled = jnp.any(matches, axis=1)
    return source_rows, filled


def token_scale(route_rows, prob_rows, length_row, mask_row, margin_row, loss_scale):
    count_rows = route_rows.shape[0]
    seq_count = length_row.shape[0]
    seq_ends = jnp.cumsum(length_row).astype(jnp.int32)
    positions = jnp.arange(count_rows, dtype=jnp.int32)
    seq_index = jnp.sum((positions[:, None] >= seq_ends[None, :]).astype(jnp.int32), axis=1)
    pair_weight = mask_row.astype(jnp.float32) * jax.nn.sigmoid(-margin_row) * loss_scale
    per_seq = jnp.stack([-pair_weight, pair_weight], axis=1).reshape(-1)
    seq_ids = jnp.arange(seq_count, dtype=jnp.int32)
    seq_weight = jnp.sum(jnp.where(seq_index[:, None] == seq_ids[None, :], per_seq[None, :], jnp.float32(0.0)), axis=1)
    router_weight = jnp.sum(jnp.where(route_rows == 0, prob_rows, jnp.float32(0.0)), axis=1)
    return seq_weight * router_weight


def backward(gate_value, up_value, cotangent):
    sigmoid_gate = jax.nn.sigmoid(gate_value)
    grad_up = (cotangent * gate_value * sigmoid_gate).astype(jnp.bfloat16)
    grad_gate = (cotangent * up_value * sigmoid_gate * (1.0 + gate_value * (1.0 - sigmoid_gate))).astype(jnp.bfloat16)
    return grad_gate, grad_up


def reference(tokens, routes, router_prob, lengths, pair_mask, margins, hidden_grad, gate_weight, up_weight):
    total_pairs = jnp.sum(pair_mask.astype(jnp.float32))
    loss_scale = (N_FSDP * PAIRS) / total_pairs
    gate_full = gate_weight.astype(jnp.float32)
    up_full = up_weight.astype(jnp.float32)

    def shard(pieces):
        tok_rows, route_rows, prob_rows, length_row, mask_row, margin_row, grad_rows = pieces
        coef_tok = token_scale(route_rows, prob_rows, length_row, mask_row, margin_row, loss_scale)
        source_rows, filled = slot_table(route_rows, CAP)
        slot_rows = jnp.where(filled[:, None], tok_rows[source_rows], jnp.zeros((), jnp.bfloat16))
        coefficient = jnp.where(filled, coef_tok[source_rows], jnp.float32(0.0))
        cotangent = coefficient[:, None] * grad_rows[source_rows].astype(jnp.float32)
        gate_value = jnp.dot(slot_rows, gate_weight, preferred_element_type=jnp.float32)
        up_value = jnp.dot(slot_rows, up_weight, preferred_element_type=jnp.float32)
        grad_gate, grad_up = backward(gate_value, up_value, cotangent)
        total = jnp.einsum("cf,df->cd", grad_gate.astype(jnp.float32), gate_full) + jnp.einsum("cf,df->cd", grad_up.astype(jnp.float32), up_full)
        return total

    outputs = lax.map(shard, (tokens.reshape(N_FSDP, TOK_DEV, D), routes.reshape(N_FSDP, TOK_DEV, 2), router_prob.reshape(N_FSDP, TOK_DEV, 2), lengths, pair_mask, margins, hidden_grad.reshape(N_FSDP, TOK_DEV, FF)))
    return outputs.reshape(N_FSDP * CAP, D)
```

```python
import jax
import jax.numpy as jnp
from jax import lax
from jax.sharding import Mesh, PartitionSpec as P

CAP = 160
SHIFT = 2.0**19


def slot_matrix(route_rows, capacity):
    routed = jnp.any(route_rows == 0, axis=1)
    slot_of = jnp.cumsum(routed.astype(jnp.int32)) - 1
    slots = jnp.arange(capacity, dtype=jnp.int32)
    return (slot_of[None, :] == slots[:, None]) & routed[None, :]


def token_scale(route_rows, prob_rows, length_row, mask_row, margin_row):
    count_rows = route_rows.shape[0]
    seq_count = length_row.shape[0]
    seq_ends = jnp.cumsum(length_row)
    positions = jnp.arange(count_rows, dtype=jnp.int32)
    seq_index = jnp.sum((positions[:, None] >= seq_ends[None, :]).astype(jnp.int32), axis=1)
    pair_weight = mask_row.astype(jnp.float32) * jax.nn.sigmoid(-margin_row)
    per_seq = jnp.stack([-pair_weight, pair_weight], axis=1).reshape(-1)
    seq_ids = jnp.arange(seq_count, dtype=jnp.int32)
    seq_weight = jnp.sum(
        jnp.where(seq_index[:, None] == seq_ids[None, :], per_seq[None, :], jnp.float32(0.0)),
        axis=1,
    )
    router_weight = jnp.sum(jnp.where(route_rows == 0, prob_rows, jnp.float32(0.0)), axis=1)
    return seq_weight * router_weight


def backward(gate_value, up_value, cotangent):
    sigmoid_gate = jax.nn.sigmoid(gate_value)
    grad_up = (cotangent * gate_value * sigmoid_gate).astype(jnp.bfloat16)
    grad_gate = (
        cotangent * up_value * sigmoid_gate * (1.0 + gate_value * (1.0 - sigmoid_gate))
    ).astype(jnp.bfloat16)
    return (grad_gate, grad_up)


def swap(value, axis):
    return lax.ppermute(value, axis, [(0, 1), (1, 0)])


def body(
    tokens, routes, router_prob, lengths, pair_mask, margins, hidden_grad, gate_weight, up_weight
):
    n_y, n_z = lax.axis_size("y"), lax.axis_size("z")
    rows, units = gate_weight.shape
    pairs = margins.shape[1]
    own = jnp.concatenate([gate_weight, up_weight], axis=1).astype(jnp.float32) * SHIFT
    count = jnp.sum(pair_mask.astype(jnp.float32))
    own = jnp.concatenate([own, jnp.broadcast_to(count, (16, 2 * units))]).astype(jnp.float16)
    other = swap(own, "xh")
    first = lax.axis_index("xh") == 0
    both = jnp.stack([jnp.where(first, own, other), jnp.where(first, other, own)])
    whole = lax.all_gather(both, ("y", "core"), axis=0, tiled=False)
    whole = whole.reshape(n_y, 2, 2, rows + 16, 2 * units)
    total_pairs = jnp.sum(whole[:, :, :, rows, 0].astype(jnp.float32))
    loss_scale = whole.shape[0] * 4 * pairs / total_pairs
    weight = whole[:, :, :, :rows].transpose(0, 2, 1, 3, 4).astype(jnp.bfloat16)
    weight = weight.reshape(n_y * 4 * rows, 2 * units)

    taken = slot_matrix(routes, CAP)
    picks = taken.astype(jnp.bfloat16)
    slot_rows = jnp.dot(picks, tokens, preferred_element_type=jnp.float32).astype(jnp.bfloat16)
    grad_rows = jnp.dot(picks, hidden_grad, preferred_element_type=jnp.float32)
    coef_tok = token_scale(routes, router_prob, lengths[0], pair_mask[0], margins[0])
    coefficient = jnp.sum(jnp.where(taken, coef_tok[None, :], jnp.float32(0.0)), axis=1)

    cotangent = (coefficient * loss_scale)[:, None] * grad_rows
    value = jnp.dot(slot_rows, weight, preferred_element_type=jnp.float32) * (1.0 / SHIFT)
    grads = jnp.concatenate(backward(value[:, :units], value[:, units:], cotangent), axis=1)

    mine = lax.axis_index("xl")
    width = weight.shape[0] // (2 * n_z)
    columns = weight.reshape(n_z, 2, width, 2 * units)

    def partial(side):
        part = lax.dynamic_index_in_dim(columns, side, 1, keepdims=False)
        part = part.reshape(n_z * width, 2 * units)
        out = lax.dot_general(
            grads, part, (((1,), (1,)), ((), ())), preferred_element_type=jnp.float32
        )
        return out.reshape(CAP, n_z, width).transpose(1, 0, 2)

    received = swap(partial(1 - mine).astype(jnp.bfloat16), "xl")
    summed = (partial(mine) + received.astype(jnp.float32)).astype(jnp.bfloat16)
    pieces = lax.all_to_all(summed, "z", 0, 0)
    return jnp.sum(pieces.astype(jnp.float32), axis=0) * (1.0 / SHIFT)


def solution(mesh):
    n_dp, n_fsdp = mesh.devices.shape
    fine = Mesh(
        mesh.devices.reshape(n_dp // 2, 2, n_fsdp // 4, 2, 2), ("z", "xl", "y", "xh", "core")
    )
    dp, fsdp = ("z", "xl"), ("y", "xh", "core")
    placed = (P(fsdp, None),) * 6 + (P(fsdp, dp),) * 3
    return jax.shard_map(
        body, mesh=fine, in_specs=placed, out_specs=P(fsdp, dp), check_vma=False
    )
```

```python
import jax
import jax.numpy as jnp
from jax import lax
from jax.sharding import Mesh, PartitionSpec as P

CAP = 160
SHIFT = 2.0**19


def slot_matrix(route_rows, capacity):
    routed = jnp.any(route_rows == 0, axis=1)
    slot_of = jnp.cumsum(routed.astype(jnp.int32)) - 1
    slots = jnp.arange(capacity, dtype=jnp.int32)
    return (slot_of[None, :] == slots[:, None]) & routed[None, :]


def token_scale(route_rows, prob_rows, length_row, mask_row, margin_row):
    count_rows = route_rows.shape[0]
    seq_count = length_row.shape[0]
    seq_ends = jnp.cumsum(length_row)
    positions = jnp.arange(count_rows, dtype=jnp.int32)
    seq_index = jnp.sum((positions[:, None] >= seq_ends[None, :]).astype(jnp.int32), axis=1)
    pair_weight = mask_row.astype(jnp.float32) * jax.nn.sigmoid(-margin_row)
    per_seq = jnp.stack([-pair_weight, pair_weight], axis=1).reshape(-1)
    seq_ids = jnp.arange(seq_count, dtype=jnp.int32)
    seq_weight = jnp.sum(
        jnp.where(seq_index[:, None] == seq_ids[None, :], per_seq[None, :], jnp.float32(0.0)),
        axis=1,
    )
    router_weight = jnp.sum(jnp.where(route_rows == 0, prob_rows, jnp.float32(0.0)), axis=1)
    return seq_weight * router_weight


def backward(gate_value, up_value, cotangent):
    sigmoid_gate = jax.nn.sigmoid(gate_value)
    grad_up = (cotangent * gate_value * sigmoid_gate).astype(jnp.bfloat16)
    grad_gate = (
        cotangent * up_value * sigmoid_gate * (1.0 + gate_value * (1.0 - sigmoid_gate))
    ).astype(jnp.bfloat16)
    return (grad_gate, grad_up)


def swap(value, axis):
    return lax.ppermute(value, axis, [(0, 1), (1, 0)])


def half_of(value, which, axis):
    size = value.shape[axis] // 2
    low = lax.slice_in_dim(value, 0, size, axis=axis)
    high = lax.slice_in_dim(value, size, 2 * size, axis=axis)
    return jnp.where(which == 0, low, high)


def in_order(mine, theirs, which):
    return jnp.where(which == 0, jnp.stack([mine, theirs]), jnp.stack([theirs, mine]))


def body(
    tokens, routes, router_prob, lengths, pair_mask, margins, hidden_grad, gate_weight, up_weight
):
    n_y, n_z = lax.axis_size("y"), lax.axis_size("z")
    core, mine, z = lax.axis_index("core"), lax.axis_index("xl"), lax.axis_index("z")
    rows, units = gate_weight.shape
    pairs = margins.shape[1]
    tail = 16
    count = jnp.sum(pair_mask.astype(jnp.float32))

    def packed(which):
        part = [half_of(gate_weight, which, 1), half_of(up_weight, which, 1)]
        part = jnp.concatenate(part, axis=1).astype(jnp.float32) * SHIFT
        return jnp.concatenate([part, jnp.broadcast_to(count, (tail, units))]).astype(jnp.float16)

    pair = in_order(packed(core), swap(packed(1 - core), "core"), core)
    four = in_order(pair, swap(pair, "xh"), lax.axis_index("xh"))
    chip_count = jnp.sum(four[:, :, rows:].astype(jnp.float32), axis=(0, 1)).astype(jnp.float16)
    sent = jnp.concatenate([four[:, :, :rows].reshape(4 * rows, units), chip_count])
    whole = lax.all_gather(sent, "y", axis=0, tiled=False)
    total_pairs = jnp.sum(whole[:, 4 * rows, 0].astype(jnp.float32))
    loss_scale = n_y * 4 * pairs / total_pairs
    weight = whole[:, : 4 * rows].astype(jnp.bfloat16).reshape(n_y * 4 * rows, units)

    taken = slot_matrix(routes, CAP)
    picks = taken.astype(jnp.bfloat16)
    slot_rows = jnp.dot(picks, tokens, preferred_element_type=jnp.float32).astype(jnp.bfloat16)
    grad_rows = jnp.dot(picks, hidden_grad, preferred_element_type=jnp.float32)
    coef_tok = token_scale(routes, router_prob, lengths[0], pair_mask[0], margins[0])
    coefficient = jnp.sum(jnp.where(taken, coef_tok[None, :], jnp.float32(0.0)), axis=1)
    cotangent = coefficient[:, None] * grad_rows
    slot_rows = jnp.concatenate([slot_rows, swap(slot_rows, "core")])
    cotangent = jnp.concatenate(
        [half_of(cotangent, core, 1), swap(half_of(cotangent, 1 - core, 1), "core")]
    )

    value = jnp.dot(slot_rows, weight, preferred_element_type=jnp.float32) * (1.0 / SHIFT)
    grads = jnp.concatenate(
        backward(value[:, : units // 2], value[:, units // 2 :], cotangent * loss_scale), axis=1
    )

    width = weight.shape[0] // (2 * n_z)
    columns = weight.reshape(n_z, 2, width, units)

    def partial(left, side):
        part = lax.dynamic_index_in_dim(columns, side, 1, keepdims=False)
        part = part.reshape(n_z * width, units)
        out = lax.dot_general(
            left, part, (((1,), (1,)), ((), ())), preferred_element_type=jnp.float32
        )
        return out.reshape(CAP, n_z, width).transpose(1, 0, 2)

    def chip_sum(side):
        return swap(partial(grads[CAP:], side), "core") + partial(grads[:CAP], side)

    received = swap(chip_sum(1 - mine).astype(jnp.bfloat16), "xl")
    total = chip_sum(mine) + received.astype(jnp.float32)

    place, group = z % 3, z // 3
    total = total.reshape(n_z // 3, 3, CAP, width)
    kept = lax.dynamic_index_in_dim(total, place, 1, keepdims=False)
    for step in (1, 2):
        piece = lax.dynamic_index_in_dim(total, (place + step) % 3, 1, keepdims=False)
        route = [(i, i // 3 * 3 + (i + step) % 3) for i in range(n_z)]
        kept += lax.ppermute(piece.astype(jnp.bfloat16), "z", route).astype(jnp.float32)
    groups = n_z // 3
    result = lax.dynamic_index_in_dim(kept, group, 0, keepdims=False)
    for step in range(1, groups):
        piece = lax.dynamic_index_in_dim(kept, (group + step) % groups, 0, keepdims=False)
        route = [(i, (i + 3 * step) % n_z) for i in range(n_z)]
        result += lax.ppermute(piece.astype(jnp.bfloat16), "z", route).astype(jnp.float32)
    return result * (1.0 / SHIFT)


def solution(mesh):
    n_dp, n_fsdp = mesh.devices.shape
    fine = Mesh(
        mesh.devices.reshape(n_dp // 2, 2, n_fsdp // 4, 2, 2), ("z", "xl", "y", "xh", "core")
    )
    dp, fsdp = ("z", "xl"), ("y", "xh", "core")
    placed = (P(fsdp, None),) * 6 + (P(fsdp, dp),) * 3
    return jax.shard_map(
        body, mesh=fine, in_specs=placed, out_specs=P(fsdp, dp), check_vma=False
    )
```

```python
import jax
import jax.numpy as jnp
from jax import lax
from jax.sharding import Mesh, PartitionSpec as P

CAP = 160
SHIFT = 2.0**19


def slot_matrix(route_rows, capacity):
    routed = jnp.any(route_rows == 0, axis=1)
    slot_of = jnp.cumsum(routed.astype(jnp.int32)) - 1
    slots = jnp.arange(capacity, dtype=jnp.int32)
    return (slot_of[None, :] == slots[:, None]) & routed[None, :]


def token_scale(route_rows, prob_rows, length_row, mask_row, margin_row):
    count_rows = route_rows.shape[0]
    seq_count = length_row.shape[0]
    seq_ends = jnp.cumsum(length_row)
    positions = jnp.arange(count_rows, dtype=jnp.int32)
    seq_index = jnp.sum((positions[:, None] >= seq_ends[None, :]).astype(jnp.int32), axis=1)
    pair_weight = mask_row.astype(jnp.float32) * jax.nn.sigmoid(-margin_row)
    per_seq = jnp.stack([-pair_weight, pair_weight], axis=1).reshape(-1)
    seq_ids = jnp.arange(seq_count, dtype=jnp.int32)
    seq_weight = jnp.sum(
        jnp.where(seq_index[:, None] == seq_ids[None, :], per_seq[None, :], jnp.float32(0.0)),
        axis=1,
    )
    router_weight = jnp.sum(jnp.where(route_rows == 0, prob_rows, jnp.float32(0.0)), axis=1)
    return seq_weight * router_weight


def backward(gate_value, up_value, cotangent):
    sigmoid_gate = jax.nn.sigmoid(gate_value)
    grad_up = (cotangent * gate_value * sigmoid_gate).astype(jnp.bfloat16)
    grad_gate = (
        cotangent * up_value * sigmoid_gate * (1.0 + gate_value * (1.0 - sigmoid_gate))
    ).astype(jnp.bfloat16)
    return (grad_gate, grad_up)


def swap(value, axis):
    return lax.ppermute(value, axis, [(0, 1), (1, 0)])


def half_of(value, which, axis):
    size = value.shape[axis] // 2
    low = lax.slice_in_dim(value, 0, size, axis=axis)
    high = lax.slice_in_dim(value, size, 2 * size, axis=axis)
    return jnp.where(which == 0, low, high)


def in_order(mine, theirs, which):
    return jnp.where(which == 0, jnp.stack([mine, theirs]), jnp.stack([theirs, mine]))


def body(
    tokens, routes, router_prob, lengths, pair_mask, margins, hidden_grad, gate_weight, up_weight
):
    n_y, n_z = lax.axis_size("y"), lax.axis_size("z")
    core, mine, z = lax.axis_index("core"), lax.axis_index("xl"), lax.axis_index("z")
    rows, units = gate_weight.shape
    pairs = margins.shape[1]
    tail = 16
    mask_rows = jnp.pad(pair_mask.astype(jnp.float16), ((0, tail - 1), (0, units - pairs)))

    def packed(which):
        low = which * (units // 2)
        part = [lax.slice_in_dim(w, low, low + units // 2, axis=1) for w in (gate_weight, up_weight)]
        part = (jnp.concatenate(part, axis=1).astype(jnp.float32) * SHIFT).astype(jnp.float16)
        return jnp.concatenate([part, mask_rows])

    own = jnp.stack([packed(0), packed(1)])
    pair = in_order(own, swap(own, "xh"), lax.axis_index("xh"))
    kept = lax.dynamic_index_in_dim(pair, core, 1, keepdims=False)
    given = lax.dynamic_index_in_dim(pair, 1 - core, 1, keepdims=False)
    four = in_order(kept, swap(given, "core"), core).transpose(1, 0, 2, 3)
    chip_mask = jnp.sum(four[:, :, rows:].astype(jnp.float32), axis=(0, 1)).astype(jnp.float16)
    sent = jnp.concatenate([four[:, :, :rows].reshape(4 * rows, units), chip_mask])

    taken = slot_matrix(routes, CAP)
    picks = taken.astype(jnp.bfloat16)
    slot_rows = jnp.dot(picks, tokens, preferred_element_type=jnp.float32).astype(jnp.bfloat16)
    grad_rows = jnp.dot(picks, hidden_grad, preferred_element_type=jnp.float32)
    coef_tok = token_scale(routes, router_prob, lengths[0], pair_mask[0], margins[0])
    coefficient = jnp.sum(jnp.where(taken, coef_tok[None, :], jnp.float32(0.0)), axis=1)
    cotangent = coefficient[:, None] * grad_rows
    their_rows = swap(slot_rows, "core")
    their_cotangent = swap(half_of(cotangent, 1 - core, 1), "core")
    cotangent = half_of(cotangent, core, 1)
    sent, slot_rows, cotangent, their_rows, their_cotangent = lax.optimization_barrier(
        (sent, slot_rows, cotangent, their_rows, their_cotangent)
    )

    whole = lax.all_gather(sent, "y", axis=0, tiled=False)
    total_pairs = jnp.sum(whole[:, 4 * rows, :pairs].astype(jnp.float32))
    loss_scale = n_y * 4 * pairs / total_pairs
    weight = whole[:, : 4 * rows].astype(jnp.bfloat16).reshape(n_y * 4 * rows, units)

    def slot_gradients(left, weight, cotangent):
        value = jnp.dot(left, weight, preferred_element_type=jnp.float32) * (1.0 / SHIFT)
        gate_value, up_value = value[:, : units // 2], value[:, units // 2 :]
        return jnp.concatenate(backward(gate_value, up_value, cotangent * loss_scale), axis=1)

    their_grads = slot_gradients(their_rows, weight, their_cotangent)

    width = weight.shape[0] // (4 * n_z)
    columns = weight.reshape(n_z, 2, 2, width, units)
    place, group, groups = z % 3, z // 3, n_z // 3

    def partial(left, part):
        out = lax.dot_general(
            left,
            part.reshape(-1, units),
            (((1,), (1,)), ((), ())),
            preferred_element_type=jnp.float32,
        )
        return out.reshape(CAP, -1, width).transpose(1, 0, 2)

    def pick(value, index, axis):
        return lax.dynamic_index_in_dim(value, index, axis, keepdims=False)

    def send(value, axis, route):
        return lax.ppermute(value.astype(jnp.bfloat16), axis, route).astype(jnp.float32)

    def three(value):
        value = value.reshape(groups, 3, *value.shape[1:])
        moved = []
        for step in (1, 2):
            route = [(i, i // 3 * 3 + (i + step) % 3) for i in range(n_z)]
            moved.append(send(pick(value, (place + step) % 3, 1), "z", route))
        return pick(value, place, 1) + moved[0] + moved[1]

    across = [(0, 1), (1, 0)]
    part = pick(columns[:, :, 0], 1 - mine, 1)
    theirs = swap(partial(their_grads, part), "core")
    own_grads = slot_gradients(slot_rows, weight, cotangent)
    leaving = (partial(own_grads, part) + theirs).astype(jnp.bfloat16)
    leaving, own_grads, their_grads = lax.optimization_barrier((leaving, own_grads, their_grads))
    arrived = send(leaving, "xl", across)
    part = columns[:, :, 1]
    second = swap(partial(their_grads, part), "core") + partial(own_grads, part)
    second = three(second.reshape(n_z, 2, CAP, width))
    part = pick(columns[:, :, 0], mine, 1)
    first = swap(partial(their_grads, part), "core") + partial(own_grads, part) + arrived
    second = pick(second, mine, 1) + send(pick(second, 1 - mine, 1), "xl", across)
    first = three(first)
    total = jnp.concatenate([first, second], axis=2)
    result = pick(total, group, 0)
    for step in range(1, groups):
        route = [(i, (i + 3 * step) % n_z) for i in range(n_z)]
        result += send(pick(total, (group + step) % groups, 0), "z", route)
    return result * (1.0 / SHIFT)


def solution(mesh):
    n_dp, n_fsdp = mesh.devices.shape
    fine = Mesh(
        mesh.devices.reshape(n_dp // 2, 2, n_fsdp // 4, 2, 2), ("z", "xl", "y", "xh", "core")
    )
    dp, fsdp = ("z", "xl"), ("y", "xh", "core")
    placed = (P(fsdp, None),) * 6 + (P(fsdp, dp),) * 3
    return jax.shard_map(
        body, mesh=fine, in_specs=placed, out_specs=P(fsdp, dp), check_vma=False
    )
```

```python
import jax
import jax.numpy as jnp
from jax import lax
from jax.sharding import Mesh, PartitionSpec as P

CAP = 160
SHIFT = 2.0**19


def slot_matrix(route_rows, capacity):
    routed = jnp.any(route_rows == 0, axis=1)
    slot_of = jnp.cumsum(routed.astype(jnp.int32)) - 1
    slots = jnp.arange(capacity, dtype=jnp.int32)
    return (slot_of[None, :] == slots[:, None]) & routed[None, :]


def token_scale(route_rows, prob_rows, length_row, mask_row, margin_row):
    count_rows = route_rows.shape[0]
    seq_count = length_row.shape[0]
    seq_ends = jnp.cumsum(length_row)
    positions = jnp.arange(count_rows, dtype=jnp.int32)
    seq_index = jnp.sum((positions[:, None] >= seq_ends[None, :]).astype(jnp.int32), axis=1)
    pair_weight = mask_row.astype(jnp.float32) * jax.nn.sigmoid(-margin_row)
    per_seq = jnp.stack([-pair_weight, pair_weight], axis=1).reshape(-1)
    seq_ids = jnp.arange(seq_count, dtype=jnp.int32)
    seq_weight = jnp.sum(
        jnp.where(seq_index[:, None] == seq_ids[None, :], per_seq[None, :], jnp.float32(0.0)),
        axis=1,
    )
    router_weight = jnp.sum(jnp.where(route_rows == 0, prob_rows, jnp.float32(0.0)), axis=1)
    return seq_weight * router_weight


def backward(gate_value, up_value, cotangent):
    sigmoid_gate = jax.nn.sigmoid(gate_value)
    grad_up = (cotangent * gate_value * sigmoid_gate).astype(jnp.bfloat16)
    grad_gate = (
        cotangent * up_value * sigmoid_gate * (1.0 + gate_value * (1.0 - sigmoid_gate))
    ).astype(jnp.bfloat16)
    return (grad_gate, grad_up)


def swap(value, axis):
    return lax.ppermute(value, axis, [(0, 1), (1, 0)])


def half_of(value, which, axis):
    size = value.shape[axis] // 2
    low = lax.slice_in_dim(value, 0, size, axis=axis)
    high = lax.slice_in_dim(value, size, 2 * size, axis=axis)
    return jnp.where(which == 0, low, high)


def in_order(mine, theirs, which):
    return jnp.stack([jnp.where(which == 0, mine, theirs), jnp.where(which == 0, theirs, mine)])


def body(
    tokens, routes, router_prob, lengths, pair_mask, margins, hidden_grad, gate_weight, up_weight
):
    n_y, n_z = lax.axis_size("y"), lax.axis_size("z")
    core, mine, z = lax.axis_index("core"), lax.axis_index("xl"), lax.axis_index("z")
    rows, units = gate_weight.shape
    pairs = margins.shape[1]
    tail = 16
    mask_rows = jnp.pad(pair_mask.astype(jnp.float16), ((0, tail - 1), (0, units - pairs)))

    def packed(which):
        part = [half_of(gate_weight, which, 1), half_of(up_weight, which, 1)]
        part = (jnp.concatenate(part, axis=1).astype(jnp.float32) * SHIFT).astype(jnp.float16)
        return jnp.concatenate([part, mask_rows])

    pair = in_order(packed(core), swap(packed(1 - core), "core"), core)
    chip_rows = pair[:, :rows].reshape(2 * rows, units)
    chip_mask = jnp.sum(pair[:, rows:].astype(jnp.float32), axis=0).astype(jnp.float16)
    late = 2 * rows // 3
    crossed = swap(jnp.concatenate([chip_rows[late:], chip_mask]), "xh")
    crossed_mask = crossed[2 * rows - late :].astype(jnp.float32) + chip_mask.astype(jnp.float32)
    crossed = jnp.concatenate([crossed[: 2 * rows - late], crossed_mask.astype(jnp.float16)])


    taken = slot_matrix(routes, CAP)
    picks = taken.astype(jnp.bfloat16)
    slot_rows = jnp.dot(picks, tokens, preferred_element_type=jnp.float32).astype(jnp.bfloat16)
    grad_rows = jnp.dot(picks, hidden_grad, preferred_element_type=jnp.float32)
    coef_tok = token_scale(routes, router_prob, lengths[0], pair_mask[0], margins[0])
    coefficient = jnp.sum(jnp.where(taken, coef_tok[None, :], jnp.float32(0.0)), axis=1)
    cotangent = coefficient[:, None] * grad_rows
    their_rows = swap(slot_rows, "core")
    their_cotangent = swap(half_of(cotangent, 1 - core, 1), "core")
    cotangent = half_of(cotangent, core, 1)
    chip_rows, slot_rows, cotangent, their_rows, their_cotangent = lax.optimization_barrier(
        (chip_rows, slot_rows, cotangent, their_rows, their_cotangent)
    )

    whole = lax.all_gather(chip_rows, "y", axis=0, tiled=False)
    crossed, whole = lax.optimization_barrier((crossed, whole))
    after = swap(whole[:, :late], "xh")
    before = lax.all_gather(crossed, "y", axis=0, tiled=False)
    total_pairs = jnp.sum(before[:, 2 * rows - late, :pairs].astype(jnp.float32))
    loss_scale = n_y * 4 * pairs / total_pairs
    other = jnp.concatenate([after, before[:, : 2 * rows - late]], axis=1)
    weight = in_order(whole, other, lax.axis_index("xh")).astype(jnp.bfloat16)
    weight = weight.transpose(1, 0, 2, 3).reshape(n_y * 4 * rows, units)

    def slot_gradients(left, weight, cotangent):
        value = jnp.dot(left, weight, preferred_element_type=jnp.float32) * (1.0 / SHIFT)
        gate_value, up_value = value[:, : units // 2], value[:, units // 2 :]
        return jnp.concatenate(backward(gate_value, up_value, cotangent * loss_scale), axis=1)

    their_grads = slot_gradients(their_rows, weight, their_cotangent)

    width = weight.shape[0] // (4 * n_z)
    columns = weight.reshape(n_z, 2, 2, width, units)
    place, group, groups = z % 3, z // 3, n_z // 3

    def partial(left, part):
        out = lax.dot_general(
            left,
            part.reshape(-1, units),
            (((1,), (1,)), ((), ())),
            preferred_element_type=jnp.float32,
        )
        return out.reshape(CAP, -1, width).transpose(1, 0, 2)

    def pick(value, index, axis):
        return lax.dynamic_index_in_dim(value, index, axis, keepdims=False)

    def send(value, axis, route):
        return lax.ppermute(value.astype(jnp.bfloat16), axis, route).astype(jnp.float32)

    def three(value):
        value = value.reshape(groups, 3, *value.shape[1:])
        moved = []
        for step in (1, 2):
            route = [(i, i // 3 * 3 + (i + step) % 3) for i in range(n_z)]
            moved.append(send(pick(value, (place + step) % 3, 1), "z", route))
        return pick(value, place, 1) + moved[0] + moved[1]

    across = [(0, 1), (1, 0)]
    part = pick(columns[:, :, 0], 1 - mine, 1)
    theirs = swap(partial(their_grads, part), "core")
    own_grads = slot_gradients(slot_rows, weight, cotangent)
    leaving = (partial(own_grads, part) + theirs).astype(jnp.bfloat16)
    leaving, own_grads, their_grads = lax.optimization_barrier((leaving, own_grads, their_grads))
    arrived = send(leaving, "xl", across)
    part = columns[:, :, 1]
    second = swap(partial(their_grads, part), "core") + partial(own_grads, part)
    second = three(second.reshape(n_z, 2, CAP, width))
    part = pick(columns[:, :, 0], mine, 1)
    first = swap(partial(their_grads, part), "core") + partial(own_grads, part) + arrived
    second = pick(second, mine, 1) + send(pick(second, 1 - mine, 1), "xl", across)
    first = three(first)
    total = jnp.concatenate([first, second], axis=2)
    result = pick(total, group, 0)
    for step in range(1, groups):
        route = [(i, (i + 3 * step) % n_z) for i in range(n_z)]
        result += send(pick(total, (group + step) % groups, 0), "z", route)
    return result * (1.0 / SHIFT)


def solution(mesh):
    n_dp, n_fsdp = mesh.devices.shape
    fine = Mesh(
        mesh.devices.reshape(n_dp // 2, 2, n_fsdp // 4, 2, 2), ("z", "xl", "y", "xh", "core")
    )
    dp, fsdp = ("z", "xl"), ("y", "xh", "core")
    placed = (P(fsdp, None),) * 6 + (P(fsdp, dp),) * 3
    return jax.shard_map(
        body, mesh=fine, in_specs=placed, out_specs=P(fsdp, dp), check_vma=False
    )
```

```python
import jax
import jax.numpy as jnp
from jax import lax
from jax.experimental import pallas as pl
from jax.experimental.pallas import tpu as pltpu
from jax.sharding import Mesh, PartitionSpec as P

CAP = 160
SHIFT = 2.0**19


def slot_matrix(route_rows, capacity):
    routed = jnp.any(route_rows == 0, axis=1)
    slot_of = jnp.cumsum(routed.astype(jnp.int32)) - 1
    slots = jnp.arange(capacity, dtype=jnp.int32)
    return (slot_of[None, :] == slots[:, None]) & routed[None, :]


def token_scale(route_rows, prob_rows, length_row, mask_row, margin_row):
    count_rows = route_rows.shape[0]
    seq_count = length_row.shape[0]
    seq_ends = jnp.cumsum(length_row)
    positions = jnp.arange(count_rows, dtype=jnp.int32)
    seq_index = jnp.sum((positions[:, None] >= seq_ends[None, :]).astype(jnp.int32), axis=1)
    pair_weight = mask_row.astype(jnp.float32) * jax.nn.sigmoid(-margin_row)
    per_seq = jnp.stack([-pair_weight, pair_weight], axis=1).reshape(-1)
    seq_ids = jnp.arange(seq_count, dtype=jnp.int32)
    seq_weight = jnp.sum(
        jnp.where(seq_index[:, None] == seq_ids[None, :], per_seq[None, :], jnp.float32(0.0)),
        axis=1,
    )
    router_weight = jnp.sum(jnp.where(route_rows == 0, prob_rows, jnp.float32(0.0)), axis=1)
    return seq_weight * router_weight


def backward(gate_value, up_value, cotangent):
    sigmoid_gate = jax.nn.sigmoid(gate_value)
    grad_up = (cotangent * gate_value * sigmoid_gate).astype(jnp.bfloat16)
    grad_gate = (
        cotangent * up_value * sigmoid_gate * (1.0 + gate_value * (1.0 - sigmoid_gate))
    ).astype(jnp.bfloat16)
    return (grad_gate, grad_up)


def swap(value, axis):
    return lax.ppermute(value, axis, [(0, 1), (1, 0)])


FREE = pl.CostEstimate(flops=0, bytes_accessed=0, transcendentals=0)
LIMIT = pltpu.CompilerParams(vmem_limit_bytes=32 * 2**20)


def rows_kernel(picks_ref, tokens_ref, out_ref):
    out = jnp.dot(picks_ref[...], tokens_ref[...], preferred_element_type=jnp.float32)
    out_ref[...] = out.astype(out_ref.dtype)


def pick_rows(picks, tokens):
    slots, depth = picks.shape
    columns = tokens.shape[1]
    block = columns // 6
    return pl.pallas_call(
        rows_kernel,
        grid=(6,),
        in_specs=[
            pl.BlockSpec((slots, depth), lambda i: (0, 0)),
            pl.BlockSpec((depth, block), lambda i: (0, i)),
        ],
        out_specs=pl.BlockSpec((slots, block), lambda i: (0, i)),
        out_shape=jax.ShapeDtypeStruct((slots, columns), tokens.dtype),
        cost_estimate=FREE,
        compiler_params=LIMIT,
    )(picks, tokens)


def partial_kernel(side_ref, left_ref, weight_ref, *refs):
    out_ref = refs[-1]
    left = left_ref[...]
    for i in range(out_ref.shape[0]):
        for j in range(out_ref.shape[1]):
            out = lax.dot_general(
                left,
                weight_ref[i, j, 0],
                (((1,), (1,)), ((), ())),
                preferred_element_type=jnp.float32,
            )
            for ref in refs[:-1]:
                out += ref[i, j]
            out_ref[i, j] = out.astype(out_ref.dtype)


def partial(left, columns, side, half, addends=(), dtype=jnp.float32):
    n_z, n_side, _, width, units = columns.shape
    sides = n_side if side is None else 1
    steps = 4
    block = n_z // steps
    slots = left.shape[0]
    chosen = jnp.zeros((1,), jnp.int32) if side is None else side.reshape(1).astype(jnp.int32)
    tile = pl.BlockSpec((block, sides, slots, width), lambda i, s: (i, 0, 0, 0))
    return pl.pallas_call(
        partial_kernel,
        grid_spec=pltpu.PrefetchScalarGridSpec(
            num_scalar_prefetch=1,
            grid=(steps,),
            in_specs=[
                pl.BlockSpec((slots, units), lambda i, s: (0, 0)),
                pl.BlockSpec(
                    (block, sides, 1, width, units), lambda i, s: (i, s[0], half, 0, 0)
                ),
            ]
            + [tile] * len(addends),
            out_specs=tile,
        ),
        out_shape=jax.ShapeDtypeStruct((n_z, sides, slots, width), dtype),
        cost_estimate=FREE,
        compiler_params=LIMIT,
    )(chosen, left, columns, *addends)


def half_of(value, which, axis):
    size = value.shape[axis] // 2
    low = lax.slice_in_dim(value, 0, size, axis=axis)
    high = lax.slice_in_dim(value, size, 2 * size, axis=axis)
    return jnp.where(which == 0, low, high)


def in_order(mine, theirs, which):
    return jnp.where(which == 0, jnp.stack([mine, theirs]), jnp.stack([theirs, mine]))


def body(
    tokens, routes, router_prob, lengths, pair_mask, margins, hidden_grad, gate_weight, up_weight
):
    n_y, n_z = lax.axis_size("y"), lax.axis_size("z")
    core, mine, z = lax.axis_index("core"), lax.axis_index("xl"), lax.axis_index("z")
    rows, units = gate_weight.shape
    pairs = margins.shape[1]
    tail = 16
    mask_rows = jnp.pad(pair_mask.astype(jnp.float16), ((0, tail - 1), (0, units - pairs)))

    def packed(which):
        low = which * (units // 2)
        part = [lax.slice_in_dim(w, low, low + units // 2, axis=1) for w in (gate_weight, up_weight)]
        part = (jnp.concatenate(part, axis=1).astype(jnp.float32) * SHIFT).astype(jnp.float16)
        return jnp.concatenate([part, mask_rows])

    own = jnp.stack([packed(0), packed(1)])
    pair = in_order(own, swap(own, "xh"), lax.axis_index("xh"))
    kept = lax.dynamic_index_in_dim(pair, core, 1, keepdims=False)
    given = lax.dynamic_index_in_dim(pair, 1 - core, 1, keepdims=False)
    four = in_order(kept, swap(given, "core"), core).transpose(1, 0, 2, 3)
    chip_mask = jnp.sum(four[:, :, rows:].astype(jnp.float32), axis=(0, 1)).astype(jnp.float16)
    sent = jnp.concatenate([four[:, :, :rows].reshape(4 * rows, units), chip_mask])

    taken = slot_matrix(routes, CAP)
    picks = taken.astype(jnp.bfloat16)
    slot_rows = pick_rows(picks, tokens)
    grad_rows = jnp.dot(picks, hidden_grad, preferred_element_type=jnp.float32)
    coef_tok = token_scale(routes, router_prob, lengths[0], pair_mask[0], margins[0])
    coefficient = jnp.sum(jnp.where(taken, coef_tok[None, :], jnp.float32(0.0)), axis=1)
    cotangent = coefficient[:, None] * grad_rows
    sent = lax.optimization_barrier((sent, slot_rows, cotangent))[0]
    their_rows = swap(slot_rows, "core")
    their_cotangent = swap(half_of(cotangent, 1 - core, 1), "core")
    cotangent = half_of(cotangent, core, 1)

    whole = lax.all_gather(sent, "y", axis=0, tiled=False)
    total_pairs = jnp.sum(whole[:, 4 * rows, :pairs].astype(jnp.float32))
    loss_scale = n_y * 4 * pairs / total_pairs
    weight = whole[:, : 4 * rows].astype(jnp.bfloat16).reshape(n_y * 4 * rows, units)

    def slot_gradients(left, weight, cotangent):
        value = jnp.dot(left, weight, preferred_element_type=jnp.float32) * (1.0 / SHIFT)
        gate_value, up_value = value[:, : units // 2], value[:, units // 2 :]
        return jnp.concatenate(backward(gate_value, up_value, cotangent * loss_scale), axis=1)

    their_grads = slot_gradients(their_rows, weight, their_cotangent)

    width = weight.shape[0] // (4 * n_z)
    columns = weight.reshape(n_z, 2, 2, width, units)
    place, group, groups = z % 3, z // 3, n_z // 3

    def pick(value, index, axis):
        return lax.dynamic_index_in_dim(value, index, axis, keepdims=False)

    def send(value, axis, route):
        return lax.ppermute(value.astype(jnp.bfloat16), axis, route).astype(jnp.float32)

    def three(value):
        value = value.reshape(groups, 3, *value.shape[1:])
        moved = []
        for step in (1, 2):
            route = [(i, i // 3 * 3 + (i + step) % 3) for i in range(n_z)]
            moved.append(send(pick(value, (place + step) % 3, 1), "z", route))
        return pick(value, place, 1) + moved[0] + moved[1]

    across = [(0, 1), (1, 0)]
    theirs = swap(partial(their_grads, columns, 1 - mine, 0), "core")
    own_grads = slot_gradients(slot_rows, weight, cotangent)
    leaving = partial(own_grads, columns, 1 - mine, 0, (theirs,), jnp.bfloat16)
    arrived = send(leaving, "xl", across)
    theirs = swap(partial(their_grads, columns, None, 1), "core")
    second = three(partial(own_grads, columns, None, 1, (theirs,)))
    theirs = swap(partial(their_grads, columns, mine, 0), "core")
    first = partial(own_grads, columns, mine, 0, (theirs,)) + arrived
    second = pick(second, mine, 1) + send(pick(second, 1 - mine, 1), "xl", across)
    first = three(first)[:, 0]
    total = jnp.concatenate([first, second], axis=2)
    result = pick(total, group, 0)
    for step in (groups // 2, *(i for i in range(1, groups) if i != groups // 2)):
        route = [(i, (i + 3 * step) % n_z) for i in range(n_z)]
        result += send(pick(total, (group + step) % groups, 0), "z", route)
    return result * (1.0 / SHIFT)


def solution(mesh):
    n_dp, n_fsdp = mesh.devices.shape
    fine = Mesh(
        mesh.devices.reshape(n_dp // 2, 2, n_fsdp // 4, 2, 2), ("z", "xl", "y", "xh", "core")
    )
    dp, fsdp = ("z", "xl"), ("y", "xh", "core")
    placed = (P(fsdp, None),) * 6 + (P(fsdp, dp),) * 3
    return jax.shard_map(
        body, mesh=fine, in_specs=placed, out_specs=P(fsdp, dp), check_vma=False
    )
```

```python
import jax
import jax.numpy as jnp
from jax import lax
from jax.experimental import pallas as pl
from jax.experimental.pallas import tpu as pltpu
from jax.sharding import Mesh, PartitionSpec as P

CAP = 160
SHIFT = 2.0**19


def slot_matrix(route_rows, capacity):
    routed = jnp.any(route_rows == 0, axis=1)
    slot_of = jnp.cumsum(routed.astype(jnp.int32)) - 1
    slots = jnp.arange(capacity, dtype=jnp.int32)
    return (slot_of[None, :] == slots[:, None]) & routed[None, :]


def token_scale(route_rows, prob_rows, length_row, mask_row, margin_row):
    count_rows = route_rows.shape[0]
    seq_count = length_row.shape[0]
    seq_ends = jnp.cumsum(length_row)
    positions = jnp.arange(count_rows, dtype=jnp.int32)
    seq_index = jnp.sum((positions[:, None] >= seq_ends[None, :]).astype(jnp.int32), axis=1)
    pair_weight = mask_row.astype(jnp.float32) * jax.nn.sigmoid(-margin_row)
    per_seq = jnp.stack([-pair_weight, pair_weight], axis=1).reshape(-1)
    seq_ids = jnp.arange(seq_count, dtype=jnp.int32)
    seq_weight = jnp.sum(
        jnp.where(seq_index[:, None] == seq_ids[None, :], per_seq[None, :], jnp.float32(0.0)),
        axis=1,
    )
    router_weight = jnp.sum(jnp.where(route_rows == 0, prob_rows, jnp.float32(0.0)), axis=1)
    return seq_weight * router_weight


def backward(gate_value, up_value, cotangent):
    sigmoid_gate = jax.nn.sigmoid(gate_value)
    grad_up = (cotangent * gate_value * sigmoid_gate).astype(jnp.bfloat16)
    grad_gate = (
        cotangent * up_value * sigmoid_gate * (1.0 + gate_value * (1.0 - sigmoid_gate))
    ).astype(jnp.bfloat16)
    return (grad_gate, grad_up)


def swap(value, axis):
    return lax.ppermute(value, axis, [(0, 1), (1, 0)])


FREE = pl.CostEstimate(flops=0, bytes_accessed=0, transcendentals=0)
LIMIT = pltpu.CompilerParams(vmem_limit_bytes=32 * 2**20)


def rows_kernel(picks_ref, tokens_ref, out_ref):
    out = jnp.dot(picks_ref[...], tokens_ref[...], preferred_element_type=jnp.float32)
    out_ref[...] = out.astype(out_ref.dtype)


def pick_rows(picks, tokens):
    slots, depth = picks.shape
    columns = tokens.shape[1]
    block = columns // 6
    return pl.pallas_call(
        rows_kernel,
        grid=(6,),
        in_specs=[
            pl.BlockSpec((slots, depth), lambda i: (0, 0)),
            pl.BlockSpec((depth, block), lambda i: (0, i)),
        ],
        out_specs=pl.BlockSpec((slots, block), lambda i: (0, i)),
        out_shape=jax.ShapeDtypeStruct((slots, columns), tokens.dtype),
        cost_estimate=FREE,
        compiler_params=LIMIT,
    )(picks, tokens)


def half_of(value, which, axis):
    size = value.shape[axis] // 2
    low = lax.slice_in_dim(value, 0, size, axis=axis)
    high = lax.slice_in_dim(value, size, 2 * size, axis=axis)
    return jnp.where(which == 0, low, high)


def in_order(mine, theirs, which):
    return jnp.where(which == 0, jnp.stack([mine, theirs]), jnp.stack([theirs, mine]))


def body(
    tokens, routes, router_prob, lengths, pair_mask, margins, hidden_grad, gate_weight, up_weight
):
    n_y, n_z = lax.axis_size("y"), lax.axis_size("z")
    core, mine, z = lax.axis_index("core"), lax.axis_index("xl"), lax.axis_index("z")
    rows, units = gate_weight.shape
    pairs = margins.shape[1]
    tail = 16
    mask_rows = jnp.pad(pair_mask.astype(jnp.float16), ((0, tail - 1), (0, units - pairs)))

    def packed(which):
        low = which * (units // 2)
        part = [lax.slice_in_dim(w, low, low + units // 2, axis=1) for w in (gate_weight, up_weight)]
        part = (jnp.concatenate(part, axis=1).astype(jnp.float32) * SHIFT).astype(jnp.float16)
        return jnp.concatenate([part, mask_rows])

    own = jnp.stack([packed(0), packed(1)])
    pair = in_order(own, swap(own, "xh"), lax.axis_index("xh"))
    kept = lax.dynamic_index_in_dim(pair, core, 1, keepdims=False)
    given = lax.dynamic_index_in_dim(pair, 1 - core, 1, keepdims=False)
    four = in_order(kept, swap(given, "core"), core).transpose(1, 0, 2, 3)
    chip_mask = jnp.sum(four[:, :, rows:].astype(jnp.float32), axis=(0, 1)).astype(jnp.float16)
    sent = jnp.concatenate([four[:, :, :rows].reshape(4 * rows, units), chip_mask])

    taken = slot_matrix(routes, CAP)
    picks = taken.astype(jnp.bfloat16)
    slot_rows = pick_rows(picks, tokens)
    grad_rows = jnp.dot(picks, hidden_grad, preferred_element_type=jnp.float32)
    coef_tok = token_scale(routes, router_prob, lengths[0], pair_mask[0], margins[0])
    coefficient = jnp.sum(jnp.where(taken, coef_tok[None, :], jnp.float32(0.0)), axis=1)
    cotangent = coefficient[:, None] * grad_rows
    their_rows = swap(slot_rows, "core")
    their_cotangent = swap(half_of(cotangent, 1 - core, 1), "core")
    cotangent = half_of(cotangent, core, 1)
    sent, _, cotangent, their_cotangent = lax.optimization_barrier(
        (sent, slot_rows, cotangent, their_cotangent)
    )

    whole = lax.all_gather(sent, "y", axis=0, tiled=False)
    total_pairs = jnp.sum(whole[:, 4 * rows, :pairs].astype(jnp.float32))
    loss_scale = n_y * 4 * pairs / total_pairs
    weight = whole[:, : 4 * rows].astype(jnp.bfloat16).reshape(n_y * 4 * rows, units)

    def slot_gradients(left, weight, cotangent):
        value = jnp.dot(left, weight, preferred_element_type=jnp.float32) * (1.0 / SHIFT)
        gate_value, up_value = value[:, : units // 2], value[:, units // 2 :]
        return jnp.concatenate(backward(gate_value, up_value, cotangent * loss_scale), axis=1)

    their_grads = slot_gradients(their_rows, weight, their_cotangent)

    width = weight.shape[0] // (4 * n_z)
    columns = weight.reshape(n_z, 2, 2, width, units)
    place, group, groups = z % 3, z // 3, n_z // 3

    def partial(left, part):
        out = lax.dot_general(
            left,
            part.reshape(-1, units),
            (((1,), (1,)), ((), ())),
            preferred_element_type=jnp.float32,
        )
        return out.reshape(CAP, -1, width).transpose(1, 0, 2)

    def pick(value, index, axis):
        return lax.dynamic_index_in_dim(value, index, axis, keepdims=False)

    def send(value, axis, route):
        return lax.ppermute(value.astype(jnp.bfloat16), axis, route).astype(jnp.float32)

    def three(value):
        value = value.reshape(groups, 3, *value.shape[1:])
        moved = []
        for step in (1, 2):
            route = [(i, i // 3 * 3 + (i + step) % 3) for i in range(n_z)]
            moved.append(send(pick(value, (place + step) % 3, 1), "z", route))
        return pick(value, place, 1) + moved[0] + moved[1]

    across = [(0, 1), (1, 0)]
    part = pick(columns[:, :, 0], 1 - mine, 1)
    theirs = swap(partial(their_grads, part), "core")
    own_grads = slot_gradients(slot_rows, weight, cotangent)
    leaving = (partial(own_grads, part) + theirs).astype(jnp.bfloat16)
    leaving, own_grads, their_grads = lax.optimization_barrier((leaving, own_grads, their_grads))
    arrived = send(leaving, "xl", across)
    part = columns[:, :, 1]
    second = swap(partial(their_grads, part), "core") + partial(own_grads, part)
    second, their_grads = lax.optimization_barrier((second, their_grads))
    second = three(second.reshape(n_z, 2, CAP, width))
    part = pick(columns[:, :, 0], mine, 1)
    first = swap(partial(their_grads, part), "core") + partial(own_grads, part) + arrived
    second = pick(second, mine, 1) + send(pick(second, 1 - mine, 1), "xl", across)
    first = three(first)
    total = jnp.concatenate([first, second], axis=2)
    result = pick(total, group, 0)
    for step in range(1, groups):
        route = [(i, (i + 3 * step) % n_z) for i in range(n_z)]
        result += send(pick(total, (group + step) % groups, 0), "z", route)
    return result * (1.0 / SHIFT)


def solution(mesh):
    n_dp, n_fsdp = mesh.devices.shape
    fine = Mesh(
        mesh.devices.reshape(n_dp // 2, 2, n_fsdp // 4, 2, 2), ("z", "xl", "y", "xh", "core")
    )
    dp, fsdp = ("z", "xl"), ("y", "xh", "core")
    placed = (P(fsdp, None),) * 6 + (P(fsdp, dp),) * 3
    return jax.shard_map(
        body, mesh=fine, in_specs=placed, out_specs=P(fsdp, dp), check_vma=False
    )
```

```python
import jax
import jax.numpy as jnp
from jax import lax
from jax.experimental import pallas as pl
from jax.experimental.pallas import tpu as pltpu
from jax.sharding import Mesh, PartitionSpec as P

CAP = 160
SHIFT = 2.0**19


def slot_matrix(route_rows, capacity):
    routed = jnp.any(route_rows == 0, axis=1)
    slot_of = jnp.cumsum(routed.astype(jnp.int32)) - 1
    slots = jnp.arange(capacity, dtype=jnp.int32)
    return (slot_of[None, :] == slots[:, None]) & routed[None, :]


def token_scale(route_rows, prob_rows, length_row, mask_row, margin_row):
    count_rows = route_rows.shape[0]
    seq_count = length_row.shape[0]
    seq_ends = jnp.cumsum(length_row)
    positions = jnp.arange(count_rows, dtype=jnp.int32)
    seq_index = jnp.sum((positions[:, None] >= seq_ends[None, :]).astype(jnp.int32), axis=1)
    pair_weight = mask_row.astype(jnp.float32) * jax.nn.sigmoid(-margin_row)
    per_seq = jnp.stack([-pair_weight, pair_weight], axis=1).reshape(-1)
    seq_ids = jnp.arange(seq_count, dtype=jnp.int32)
    seq_weight = jnp.sum(
        jnp.where(seq_index[:, None] == seq_ids[None, :], per_seq[None, :], jnp.float32(0.0)),
        axis=1,
    )
    router_weight = jnp.sum(jnp.where(route_rows == 0, prob_rows, jnp.float32(0.0)), axis=1)
    return seq_weight * router_weight


def backward(gate_value, up_value, cotangent):
    sigmoid_gate = jax.nn.sigmoid(gate_value)
    grad_up = (cotangent * gate_value * sigmoid_gate).astype(jnp.bfloat16)
    grad_gate = (
        cotangent * up_value * sigmoid_gate * (1.0 + gate_value * (1.0 - sigmoid_gate))
    ).astype(jnp.bfloat16)
    return (grad_gate, grad_up)


def swap(value, axis):
    return lax.ppermute(value, axis, [(0, 1), (1, 0)])


FREE = pl.CostEstimate(flops=0, bytes_accessed=0, transcendentals=0)
LIMIT = pltpu.CompilerParams(vmem_limit_bytes=32 * 2**20)


def rows_kernel(picks_ref, tokens_ref, out_ref):
    out = jnp.dot(picks_ref[...], tokens_ref[...], preferred_element_type=jnp.float32)
    out_ref[...] = out.astype(out_ref.dtype)


def pick_rows(picks, tokens):
    slots, depth = picks.shape
    columns = tokens.shape[1]
    block = columns // 6
    return pl.pallas_call(
        rows_kernel,
        grid=(6,),
        in_specs=[
            pl.BlockSpec((slots, depth), lambda i: (0, 0)),
            pl.BlockSpec((depth, block), lambda i: (0, i)),
        ],
        out_specs=pl.BlockSpec((slots, block), lambda i: (0, i)),
        out_shape=jax.ShapeDtypeStruct((slots, columns), tokens.dtype),
        cost_estimate=FREE,
        compiler_params=LIMIT,
    )(picks, tokens)


def half_of(value, which, axis):
    size = value.shape[axis] // 2
    low = lax.slice_in_dim(value, 0, size, axis=axis)
    high = lax.slice_in_dim(value, size, 2 * size, axis=axis)
    return jnp.where(which == 0, low, high)


def in_order(mine, theirs, which):
    return jnp.where(which == 0, jnp.stack([mine, theirs]), jnp.stack([theirs, mine]))


def body(
    tokens, routes, router_prob, lengths, pair_mask, margins, hidden_grad, gate_weight, up_weight
):
    n_y, n_z = lax.axis_size("y"), lax.axis_size("z")
    core, mine, z = lax.axis_index("core"), lax.axis_index("xl"), lax.axis_index("z")
    rows, units = gate_weight.shape
    pairs = margins.shape[1]
    tail = 16
    mask_rows = jnp.pad(pair_mask.astype(jnp.float16), ((0, tail - 1), (0, units - pairs)))

    def packed(which):
        low = which * (units // 2)
        part = [lax.slice_in_dim(w, low, low + units // 2, axis=1) for w in (gate_weight, up_weight)]
        part = (jnp.concatenate(part, axis=1).astype(jnp.float32) * SHIFT).astype(jnp.float16)
        return jnp.concatenate([part, mask_rows])

    own = jnp.stack([packed(0), packed(1)])
    pair = in_order(own, swap(own, "xh"), lax.axis_index("xh"))
    kept = lax.dynamic_index_in_dim(pair, core, 1, keepdims=False)
    given = lax.dynamic_index_in_dim(pair, 1 - core, 1, keepdims=False)
    four = in_order(kept, swap(given, "core"), core).transpose(1, 0, 2, 3)
    chip_mask = jnp.sum(four[:, :, rows:].astype(jnp.float32), axis=(0, 1)).astype(jnp.float16)
    sent = jnp.concatenate([four[:, :, :rows].reshape(4 * rows, units), chip_mask])

    taken = slot_matrix(routes, CAP)
    picks = taken.astype(jnp.bfloat16)
    slot_rows = pick_rows(picks, tokens)
    grad_rows = jnp.dot(picks, hidden_grad, preferred_element_type=jnp.float32)
    coef_tok = token_scale(routes, router_prob, lengths[0], pair_mask[0], margins[0])
    coefficient = jnp.sum(jnp.where(taken, coef_tok[None, :], jnp.float32(0.0)), axis=1)
    cotangent = coefficient[:, None] * grad_rows
    sent = lax.optimization_barrier((sent, slot_rows, cotangent))[0]
    their_rows = swap(slot_rows, "core")
    their_cotangent = swap(half_of(cotangent, 1 - core, 1), "core")
    cotangent = half_of(cotangent, core, 1)

    whole = lax.all_gather(sent, "y", axis=0, tiled=False)
    total_pairs = jnp.sum(whole[:, 4 * rows, :pairs].astype(jnp.float32))
    loss_scale = n_y * 4 * pairs / total_pairs
    weight = whole[:, : 4 * rows].astype(jnp.bfloat16).reshape(n_y * 4 * rows, units)

    def slot_gradients(left, weight, cotangent):
        value = jnp.dot(left, weight, preferred_element_type=jnp.float32) * (1.0 / SHIFT)
        gate_value, up_value = value[:, : units // 2], value[:, units // 2 :]
        return jnp.concatenate(backward(gate_value, up_value, cotangent * loss_scale), axis=1)

    their_grads = slot_gradients(their_rows, weight, their_cotangent)

    width = weight.shape[0] // (4 * n_z)
    columns = weight.reshape(n_z, 2, 2, width, units)
    place, group, groups = z % 3, z // 3, n_z // 3

    def partial(left, part):
        out = lax.dot_general(
            left,
            part.reshape(-1, units),
            (((1,), (1,)), ((), ())),
            preferred_element_type=jnp.float32,
        )
        return out.reshape(CAP, -1, width).transpose(1, 0, 2)

    def pick(value, index, axis):
        return lax.dynamic_index_in_dim(value, index, axis, keepdims=False)

    def send(value, axis, route):
        return lax.ppermute(value.astype(jnp.bfloat16), axis, route).astype(jnp.float32)

    def three(value):
        value = value.reshape(groups, 3, *value.shape[1:])
        moved = []
        for step in (1, 2):
            route = [(i, i // 3 * 3 + (i + step) % 3) for i in range(n_z)]
            moved.append(send(pick(value, (place + step) % 3, 1), "z", route))
        return pick(value, place, 1) + moved[0] + moved[1]

    across = [(0, 1), (1, 0)]
    part = pick(columns[:, :, 0], 1 - mine, 1)
    theirs = swap(partial(their_grads, part), "core")
    both = partial(their_grads, columns[:, :, 1])
    last = partial(their_grads, pick(columns[:, :, 0], mine, 1))
    slot_rows, both, last = lax.optimization_barrier((slot_rows, both, last))
    own_grads = slot_gradients(slot_rows, weight, cotangent)
    leaving = (partial(own_grads, part) + theirs).astype(jnp.bfloat16)
    arrived = send(leaving, "xl", across)
    part = columns[:, :, 1]
    second = swap(both, "core") + partial(own_grads, part)
    second = three(second.reshape(n_z, 2, CAP, width))
    part = pick(columns[:, :, 0], mine, 1)
    first = swap(last, "core") + partial(own_grads, part) + arrived
    second = pick(second, mine, 1) + send(pick(second, 1 - mine, 1), "xl", across)
    first = three(first)
    total = jnp.concatenate([first, second], axis=2)
    result = pick(total, group, 0)
    for step in range(1, groups):
        route = [(i, (i + 3 * step) % n_z) for i in range(n_z)]
        result += send(pick(total, (group + step) % groups, 0), "z", route)
    return result * (1.0 / SHIFT)


def solution(mesh):
    n_dp, n_fsdp = mesh.devices.shape
    fine = Mesh(
        mesh.devices.reshape(n_dp // 2, 2, n_fsdp // 4, 2, 2), ("z", "xl", "y", "xh", "core")
    )
    dp, fsdp = ("z", "xl"), ("y", "xh", "core")
    placed = (P(fsdp, None),) * 6 + (P(fsdp, dp),) * 3
    return jax.shard_map(
        body, mesh=fine, in_specs=placed, out_specs=P(fsdp, dp), check_vma=False
    )
```
